32 devices in a mesh: groups: 1, blk: 32 (over z, y, x, core), term: 1.
Axes of the slice: x: 2, y: 2, z: 4, core: 2. Of those that a mesh axis runs over, the one named last changes fastest.
Arguments:
- wavefunction: bfloat16 [1792, 128, 128], P(('groups', 'blk')), may hold values from -6 to 6
- left_environment: bfloat16 [224, 2, 128, 128], P(('groups', 'blk'), 'term'), may hold values from -0.5 to 0.5
- right_environment: bfloat16 [224, 2, 128, 128], P(('groups', 'blk'), 'term'), may hold values from -0.5 to 0.5
- right_sector: int32 [1792], P(('groups', 'blk')), may hold values from 0 to 223, as said below
- left_dims: int32 [224], P(('groups', 'blk')), may hold values from 32 to 128, as said below
- right_dims: int32 [224], P(('groups', 'blk')), may hold values from 32 to 128, as said below
Outputs:
- product_blocks: bfloat16 [1792, 128, 128], P(('groups', 'blk'), 'term')
The draws below stay inside these ranges and needn't reach their ends.
Inputs may be any that keep to these rules, and one draw needn't show every extreme that they name: `right_sector`: block k lies on blk index floor(k / 56); the sectors s with equal floor(s / 7) form an aligned run. At most 3 blocks of one blk index name sectors of one run, and in every draw one run is named by exactly 3 blocks of every blk index. `left_dims`: some sector has dimension exactly 128. `right_dims`: some sector has dimension exactly 128.
All inputs are finite; a program needn't handle non-finite values.
Results may differ from the reference program's by a relative error of at most 0.0059.
Values may be sent and summed in bfloat16 or wider, within the bound.
A program may use at most 128 MiB of HBM per device.

```python
import jax
import jax.numpy as jnp
from jax import lax

S = 128
TERM_DEV = 2
PER_SECTOR = 8
A_DEV = 7
BLK_DEV = 56
CAP = 3
NSEC = 224
NB = 1792
TERMS = 2
N_BLK = 32
N_TERM = 1


def draw_right_sector(key, part):
    key = jax.random.fold_in(key, 11)
    hottest = jax.random.randint(jax.random.fold_in(key, 1), (), 0, N_BLK)

    def one_source(source):
        subkey = jax.random.fold_in(key, source + 7)
        scores = jax.random.permutation(jax.random.fold_in(subkey, 1), N_BLK)
        scores = jnp.where(jnp.arange(N_BLK) == hottest, -1, scores)
        ordering = jnp.argsort(scores, stable=True)
        holders = jnp.repeat(ordering, CAP, total_repeat_length=N_BLK * CAP)[:BLK_DEV]
        holders = jax.random.permutation(jax.random.fold_in(subkey, 2), holders)
        within = jax.random.randint(jax.random.fold_in(subkey, 3), (BLK_DEV,), 0, A_DEV)
        return holders * A_DEV + within
    return jax.vmap(one_source)(jnp.arange(N_BLK)).reshape(NB).astype(jnp.int32)


def sector_sizes(key):
    values = jax.random.randint(key, (NSEC,), S // 4, S + 1)
    largest = jax.random.randint(jax.random.fold_in(key, 1), (), 0, NSEC)
    return jnp.where(jnp.arange(NSEC) == largest, S, values).astype(jnp.int32)


def draw_left_dims(key, part):
    key = jax.random.fold_in(key, 21)
    return sector_sizes(key)


def draw_right_dims(key, part):
    key = jax.random.fold_in(key, 22)
    return sector_sizes(key)


def steps_of(rng, dims, shards, smallest, high):
    level = 1.0
    for axis_at, shards_of in shards:
        draws = jax.random.uniform(jax.random.fold_in(jax.random.fold_in(rng, 6), axis_at), (shards_of,), jnp.float32, smallest / len(shards), high / len(shards))
        level = level * jnp.repeat(jnp.exp(draws), dims[axis_at] // shards_of).reshape((-1,) + (1,) * (len(dims) - 1 - axis_at))
    return level


def noise(own_key, extent, width, reach, split=(), kind=jnp.bfloat16):
    entries = width * jax.random.normal(own_key, extent, jnp.float32)
    if split:
        entries = entries * steps_of(own_key, extent, split, -0.22, 0.18)
    return jnp.clip(entries, -reach, reach).astype(kind)


def setup_inputs(seed: int = 0, part: int = 0) -> dict:
    splits = jax.random.split(jax.random.key(seed), 7)
    part_splits = jax.random.split(jax.random.fold_in(splits[6], part), 7)
    wavefunction = noise(part_splits[0], (NB, S, S), 1.0, 6.0, ((0, 32),))
    left_environment = noise(part_splits[1], (NSEC, TERMS, S, S), S ** -0.5, 0.5, ((0, 32),))
    right_environment = noise(part_splits[2], (NSEC, TERMS, S, S), S ** -0.5, 0.5, ((0, 32),))
    right_sector = draw_right_sector(jax.random.fold_in(jax.random.fold_in(splits[6], part), 71), part)
    left_dims = draw_left_dims(jax.random.fold_in(jax.random.fold_in(splits[6], part), 71), part)
    right_dims = draw_right_dims(jax.random.fold_in(jax.random.fold_in(splits[6], part), 71), part)
    return dict(wavefunction=wavefunction, left_environment=left_environment, right_environment=right_environment, right_sector=right_sector, left_dims=left_dims, right_dims=right_dims)


def reference(wavefunction, left_environment, right_environment, right_sector, left_dims, right_dims):
    row_numbers = jnp.arange(S, dtype=jnp.int32)
    per_device = BLK_DEV

    def device_blocks(device):
        leading = (device * per_device).astype(jnp.int32)
        blocks = lax.dynamic_slice_in_dim(wavefunction, leading, per_device, 0)
        sectors = lax.dynamic_slice_in_dim(right_sector, leading, per_device, 0).astype(jnp.int32)
        left_index = ((leading + jnp.arange(per_device, dtype=jnp.int32)) // PER_SECTOR).astype(jnp.int32)
        row_keep = (row_numbers[None, :] < left_dims[left_index][:, None]).astype(jnp.float32)
        col_keep = (row_numbers[None, :] < right_dims[sectors][:, None]).astype(jnp.float32)
        masked = (blocks.astype(jnp.float32) * row_keep[:, :, None]).astype(jnp.bfloat16)
        left_ops = left_environment[left_index].astype(jnp.float32)
        left_part = jnp.einsum("btij,bjk->btik", left_ops, masked.astype(jnp.float32))
        left_part = lax.optimization_barrier(left_part.astype(jnp.bfloat16)).astype(jnp.float32)
        left_part = left_part * col_keep[:, None, None, :]
        right_ops = right_environment[sectors].astype(jnp.float32)
        products = jnp.einsum("btij,btjk->btik", left_part, right_ops)
        grouped = products.reshape(per_device, N_TERM, TERM_DEV, S, S).sum(axis=2) * col_keep[:, None, None, :]
        grouped = lax.optimization_barrier(grouped.astype(jnp.bfloat16)).astype(jnp.float32)
        summed = grouped.sum(axis=1) * row_keep[:, :, None]
        return summed.astype(jnp.bfloat16)

    result = lax.map(device_blocks, jnp.arange(N_BLK, dtype=jnp.int32))
    return result.reshape(NB, S, S)
```

```python
import jax
import jax.numpy as jnp
from jax import lax
from jax.sharding import PartitionSpec as P

PER_SECTOR = 8


def keep_below(limits, extent):
    return jnp.arange(extent, dtype=jnp.int32)[None, :] < limits[:, None]


def body(wavefunction, left_environment, right_environment, right_sector, left_dims, right_dims):
    blocks_here, extent, _ = wavefunction.shape
    sectors_here, terms_here = (left_environment.shape[0], left_environment.shape[1])
    right_all = lax.all_gather(right_environment, "blk", axis=0, tiled=True)
    dims_all = lax.all_gather(right_dims, "blk", axis=0, tiled=True)
    left_index = jnp.arange(blocks_here, dtype=jnp.int32) // PER_SECTOR
    row_keep = keep_below(left_dims[left_index], extent)
    masked = jnp.where(row_keep[:, :, None], wavefunction, jnp.zeros((), jnp.bfloat16))
    grouped = masked.reshape(sectors_here, PER_SECTOR, extent, extent)
    left_part = jnp.einsum(
        "atij,apjk->aptik", left_environment, grouped, preferred_element_type=jnp.float32
    )
    left_part = left_part.astype(jnp.bfloat16).reshape(blocks_here, terms_here, extent, extent)
    col_keep = keep_below(dims_all[right_sector], extent)
    left_part = jnp.where(col_keep[:, None, None, :], left_part, jnp.zeros((), jnp.bfloat16))
    operators = right_all[right_sector]
    products = jnp.einsum(
        "ntij,ntjk->nik", left_part, operators, preferred_element_type=jnp.float32
    )
    products = jnp.where(col_keep[:, None, :], products, 0.0).astype(jnp.bfloat16)
    summed = lax.psum_scatter(
        products, "term", scatter_dimension=1, tiled=True,
    ).astype(jnp.float32)
    rows_here = summed.shape[1]
    row_numbers = lax.axis_index("term") * rows_here + jnp.arange(rows_here, dtype=jnp.int32)
    keep_rows = row_numbers[None, :] < left_dims[left_index][:, None]
    return jnp.where(keep_rows[:, :, None], summed, 0.0).astype(jnp.bfloat16)


def solution(mesh):
    placed = (
        P(("groups", "blk"), None, None),
        P(("groups", "blk"), "term", None, None),
        P(("groups", "blk"), "term", None, None),
        P(("groups", "blk")),
        P(("groups", "blk")),
        P(("groups", "blk")),
    )
    return jax.shard_map(
        body,
        mesh=mesh,
        in_specs=placed,
        out_specs=P(("groups", "blk"), "term", None),
        check_vma=False,
    )
```

```python
import functools

import jax
import jax.numpy as jnp
from jax import lax
from jax.experimental import pallas as pl
from jax.experimental.pallas import tpu as pltpu
from jax.sharding import PartitionSpec as P

PER_SECTOR = 8
VMEM_BYTES = 50 * 1024 * 1024
ROUTES = (("xzy", 2), ("yzx", 2), ("zxy", 1), ("zyx", 1))


def keep_below(limits, extent):
    return jnp.arange(extent, dtype=jnp.int32)[None, :] < limits[:, None]


def square_mask(operators, limits):
    keep = keep_below(limits, operators.shape[-1])
    keep = keep[:, None, :, None] & keep[:, None, None, :]
    return jnp.where(keep, operators, jnp.zeros((), operators.dtype))


def split_rows(rows):
    total = sum(weight for _, weight in ROUTES)
    parts, start, used = [], 0, 0
    for order, weight in ROUTES:
        used += weight
        stop = rows if used == total else rows * used // total // 16 * 16
        parts.append((order, start, stop - start))
        start = stop
    return parts


def kernel(devices, terms, psi_hbm, left_ref, right_ref, sector_ref, ldim_ref, rdim_ref, out_ref,
           gathered, psi, lmask, lpart, send_sem, recv_sem, psi_sem):
    sectors, _, extent, _ = right_ref.shape
    blocks = psi.shape[0]
    height = terms * extent
    depth = devices // 8
    me = lax.axis_index("blk")
    core, x, y, z = me % 2, (me // 2) % 2, (me // 4) % 2, me // 8

    def at(zz, yy, xx, cc):
        return zz * 8 + yy * 4 + xx * 2 + cc

    psi_copy = pltpu.make_async_copy(psi_hbm, psi, psi_sem)
    psi_copy.start()

    barrier = pltpu.get_barrier_semaphore()
    for peer in (at(z, y, x, 1 - core), at(z, y, 1 - x, core), at(z, 1 - y, x, core)):
        pl.semaphore_signal(barrier, inc=1, device_id={"blk": peer}, device_id_type=pl.DeviceIdType.MESH)

    @pl.when(z > 0)
    def _():
        pl.semaphore_signal(barrier, inc=1, device_id={"blk": me - 8}, device_id_type=pl.DeviceIdType.MESH)

    @pl.when(z < depth - 1)
    def _():
        pl.semaphore_signal(barrier, inc=1, device_id={"blk": me + 8}, device_id_type=pl.DeviceIdType.MESH)

    row_numbers = lax.broadcasted_iota(jnp.int32, (extent, extent), 0)
    col_numbers = lax.broadcasted_iota(jnp.int32, (extent, extent), 1)
    farthest = jnp.maximum(row_numbers, col_numbers)

    def mask_right(a, carry):
        keep = farthest < rdim_ref[a]
        for t in range(terms):
            gathered[me * sectors + a, pl.ds(t * extent, extent), :] = jnp.where(keep, right_ref[a, t].astype(jnp.float32), 0.0).astype(jnp.bfloat16)
        return carry

    lax.fori_loop(0, sectors, mask_right, 0)
    pl.semaphore_wait(barrier, 3 + jnp.where(z > 0, 1, 0) + jnp.where(z < depth - 1, 1, 0))

    parts = split_rows(height)

    def piece(p, origin):
        _, start, count = parts[p]
        return gathered.at[pl.ds(origin * sectors, sectors), pl.ds(start, count), :]

    sends = []

    def send(p, event, kind, origin, target, condition=None):
        def copy():
            return pltpu.make_async_remote_copy(
                src_ref=piece(p, origin), dst_ref=piece(p, origin),
                send_sem=send_sem.at[p, event, kind], recv_sem=recv_sem.at[p, origin],
                device_id={"blk": target}, device_id_type=pl.DeviceIdType.MESH)
        if condition is None:
            copy().start()
        else:
            pl.when(condition)(lambda: copy().start())
        sends.append((copy, condition))

    def wait_arrival(p, origin):
        pltpu.make_async_remote_copy(
            src_ref=piece(p, origin), dst_ref=piece(p, origin),
            send_sem=send_sem.at[p, 0, 0], recv_sem=recv_sem.at[p, origin],
            device_id={"blk": at(z, y, x, 1 - core)}, device_id_type=pl.DeviceIdType.MESH).wait_recv()

    def other(rank):
        low = z < depth // 2
        mine = jnp.where(low, z, depth - 1 - z)
        found = jnp.where(rank - 1 < mine, rank - 1, rank)
        return jnp.where(low, found, depth - 1 - found)

    def forward(p, event, origin, later, onward):
        if onward is not None:
            target_z, inside = onward
            send(p, event, 2, origin, at(target_z, y, x, core), inside)
        for dim in later:
            if dim == "z":
                send(p, event, 2, origin, me - 8, z > 0)
                send(p, event, 3, origin, me + 8, z < depth - 1)
            elif dim == "x":
                send(p, event, 0, origin, at(z, y, 1 - x, core))
            else:
                send(p, event, 1, origin, at(z, 1 - y, x, core))
        send(p, event, 4, origin, at(z, y, x, 1 - core))

    def left_sector(a):
        keep = farthest < ldim_ref[a]
        for t in range(terms):
            lmask[pl.ds(t * extent, extent), :] = jnp.where(
                keep, left_ref[a, t].astype(jnp.float32), 0.0).astype(jnp.bfloat16)

        def one(i, carry):
            k = a * PER_SECTOR + i
            both = jnp.dot(lmask[...], psi[k], preferred_element_type=jnp.float32)
            for t in range(terms):
                lpart[k, :, pl.ds(t * extent, extent)] = both[t * extent:(t + 1) * extent].astype(jnp.bfloat16)
            return carry

        lax.fori_loop(0, PER_SECTOR, one, 0, unroll=4)

    for p, (order, _, _) in enumerate(parts):
        forward(p, 0, me, order, None)
    psi_copy.wait()

    events = [(rank, dy, dx) for rank in range(depth) for dy in range(2) for dx in range(2)][1:]
    events.sort(key=lambda e: (sum(e), e))
    done = 0
    for number, (rank, dy, dx) in enumerate(events):
        origin_z = other(rank) if rank else z
        origin = at(origin_z, 1 - y if dy else y, 1 - x if dx else x, core)
        for p, (order, _, _) in enumerate(parts):
            differs = {"x": dx, "y": dy, "z": rank}
            arrived = max(i for i, dim in enumerate(order) if differs[dim])
            onward = None
            if order[arrived] == "z":
                below = origin_z < z
                onward = (jnp.where(below, z + 1, z - 1),
                          jnp.where(below, depth - 1 - z, z) > 0)
            wait_arrival(p, origin)
            forward(p, number + 1, origin, order[arrived + 1:], onward)
        if done < sectors:
            left_sector(done)
            done += 1
    for a in range(done, sectors):
        left_sector(a)

    for chip in range(devices // 2):
        for p in range(len(parts)):
            wait_arrival(p, chip * 2 + 1 - core)

    def right(k, carry):
        out_ref[k] = jnp.dot(lpart[k], gathered[sector_ref[k]], preferred_element_type=jnp.float32).astype(jnp.bfloat16)
        return carry

    lax.fori_loop(0, blocks, right, 0, unroll=4)

    for copy, condition in sends:
        if condition is None:
            copy().wait_send()
        else:
            pl.when(condition)(lambda copy=copy: copy().wait_send())


def fused(devices, wavefunction, left_environment, right_environment, right_sector, left_dims, right_dims):
    blocks, extent, _ = wavefunction.shape
    sectors, terms = left_environment.shape[:2]
    height = terms * extent
    parts = len(split_rows(height))
    vmem = pl.BlockSpec(memory_space=pltpu.VMEM)
    smem = pl.BlockSpec(memory_space=pltpu.SMEM)
    return pl.pallas_call(
        functools.partial(kernel, devices, terms),
        out_shape=jax.ShapeDtypeStruct((blocks, extent, extent), jnp.bfloat16),
        in_specs=[pl.BlockSpec(memory_space=pl.ANY), vmem, vmem, smem, smem, smem],
        out_specs=vmem,
        scratch_shapes=[
            pltpu.VMEM((devices * sectors, height, extent), jnp.bfloat16),
            pltpu.VMEM((blocks, extent, extent), jnp.bfloat16),
            pltpu.VMEM((height, extent), jnp.bfloat16),
            pltpu.VMEM((blocks, extent, height), jnp.bfloat16),
            pltpu.SemaphoreType.DMA((parts, devices // 2, 5)),
            pltpu.SemaphoreType.DMA((parts, devices)),
            pltpu.SemaphoreType.DMA,
        ],
        compiler_params=pltpu.CompilerParams(
            collective_id=0, has_side_effects=True, vmem_limit_bytes=VMEM_BYTES),
        cost_estimate=pl.CostEstimate(
            flops=4 * blocks * terms * extent ** 3, transcendentals=0,
            bytes_accessed=4 * blocks * extent * extent),
    )(wavefunction, left_environment, right_environment, right_sector, left_dims, right_dims)


def body(wavefunction, left_environment, right_environment, right_sector, left_dims, right_dims):
    devices = lax.axis_size("blk")
    blocks_here, extent, _ = wavefunction.shape
    sectors_here, terms_here = left_environment.shape[:2]
    needed = 2 * extent * extent * (terms_here * (devices + 1) * sectors_here + (3 + terms_here) * blocks_here)
    if lax.axis_size("term") == 1 and devices % 16 == 0 and needed < VMEM_BYTES * 3 // 4:
        return fused(devices, wavefunction, left_environment, right_environment, right_sector,
                     left_dims, right_dims)
    right_all = lax.all_gather(square_mask(right_environment, right_dims), "blk", axis=0, tiled=True)
    grouped = wavefunction.reshape(sectors_here, PER_SECTOR, extent, extent)
    left_part = jnp.einsum(
        "atij,apjk->aptik", square_mask(left_environment, left_dims), grouped,
        preferred_element_type=jnp.float32
    )
    left_part = left_part.astype(jnp.bfloat16).reshape(blocks_here, terms_here, extent, extent)
    products = jnp.einsum(
        "ntij,ntjk->nik", left_part, right_all[right_sector], preferred_element_type=jnp.float32
    ).astype(jnp.bfloat16)
    return lax.psum_scatter(products, "term", scatter_dimension=1, tiled=True)


def solution(mesh):
    placed = (
        P(("groups", "blk"), None, None),
        P(("groups", "blk"), "term", None, None),
        P(("groups", "blk"), "term", None, None),
        P(("groups", "blk")),
        P(("groups", "blk")),
        P(("groups", "blk")),
    )
    return jax.shard_map(
        body,
        mesh=mesh,
        in_specs=placed,
        out_specs=P(("groups", "blk"), "term", None),
        check_vma=False,
    )
```

```python
import functools

import jax
import jax.numpy as jnp
from jax import lax
from jax.experimental import pallas as pl
from jax.experimental.pallas import tpu as pltpu
from jax.sharding import PartitionSpec as P

PER_SECTOR = 8
VMEM_BYTES = 50 * 1024 * 1024
ROUTES = (("zyx", 4), ("xzy", 3))


def keep_below(limits, extent):
    return jnp.arange(extent, dtype=jnp.int32)[None, :] < limits[:, None]


def square_mask(operators, limits):
    keep = keep_below(limits, operators.shape[-1])
    keep = keep[:, None, :, None] & keep[:, None, None, :]
    return jnp.where(keep, operators, jnp.zeros((), operators.dtype))


def split_sectors(sectors):
    total = sum(weight for _, weight in ROUTES)
    parts, start, used = [], 0, 0
    for order, weight in ROUTES:
        used += weight
        stop = sectors * used // total
        parts.append((order, start, stop - start))
        start = stop
    return parts


def kernel(devices, terms, psi_hbm, left_hbm, right_hbm, sector_hbm, ldim_hbm, rdim_hbm, out_ref,
           gathered, psi, left_ref, right_ref, sector_ref, ldim_ref, rdim_ref, lmask, lpart,
           send_sem, recv_sem, load_sem):
    sectors, _, extent, _ = right_ref.shape
    blocks = psi.shape[0]
    height = terms * extent
    depth = devices // 8
    me = lax.axis_index("blk")
    core, x, y, z = me % 2, (me // 2) % 2, (me // 4) % 2, me // 8

    def at(zz, yy, xx, cc):
        return zz * 8 + yy * 4 + xx * 2 + cc

    loads = [
        pltpu.make_async_copy(source, target, load_sem.at[i])
        for i, (source, target) in enumerate((
            (rdim_hbm, rdim_ref), (right_hbm, right_ref), (left_hbm, left_ref),
            (psi_hbm, psi), (ldim_hbm, ldim_ref), (sector_hbm, sector_ref)))
    ]
    for load in loads:
        load.start()

    barrier = pltpu.get_barrier_semaphore()
    for peer in (at(z, y, x, 1 - core), at(z, y, 1 - x, core), at(z, 1 - y, x, core)):
        pl.semaphore_signal(barrier, inc=1, device_id={"blk": peer}, device_id_type=pl.DeviceIdType.MESH)

    @pl.when(z > 0)
    def _():
        pl.semaphore_signal(barrier, inc=1, device_id={"blk": me - 8}, device_id_type=pl.DeviceIdType.MESH)

    @pl.when(z < depth - 1)
    def _():
        pl.semaphore_signal(barrier, inc=1, device_id={"blk": me + 8}, device_id_type=pl.DeviceIdType.MESH)

    row_numbers = lax.broadcasted_iota(jnp.int32, (extent, extent), 0)
    col_numbers = lax.broadcasted_iota(jnp.int32, (extent, extent), 1)
    farthest = jnp.maximum(row_numbers, col_numbers)

    for load in loads[:2]:
        load.wait()

    def mask_right(a, carry):
        keep = farthest < rdim_ref[a]
        for t in range(terms):
            gathered[me * sectors + a, pl.ds(t * extent, extent), :] = jnp.where(keep, right_ref[a, t].astype(jnp.float32), 0.0).astype(jnp.bfloat16)
        return carry


    parts = split_sectors(sectors)

    def piece(p, origin):
        _, start, count = parts[p]
        return gathered.at[pl.ds(origin * sectors + start, count)]

    sends = []

    def send(p, event, kind, origin, target, condition=None):
        def copy():
            return pltpu.make_async_remote_copy(
                src_ref=piece(p, origin), dst_ref=piece(p, origin),
                send_sem=send_sem.at[p, event, kind], recv_sem=recv_sem.at[p, origin],
                device_id={"blk": target}, device_id_type=pl.DeviceIdType.MESH)
        if condition is None:
            copy().start()
        else:
            pl.when(condition)(lambda: copy().start())
        sends.append((copy, condition))

    def wait_arrival(p, origin):
        pltpu.make_async_remote_copy(
            src_ref=piece(p, origin), dst_ref=piece(p, origin),
            send_sem=send_sem.at[p, 0, 0], recv_sem=recv_sem.at[p, origin],
            device_id={"blk": at(z, y, x, 1 - core)}, device_id_type=pl.DeviceIdType.MESH).wait_recv()

    def other(rank):
        low = z < depth // 2
        mine = jnp.where(low, z, depth - 1 - z)
        found = jnp.where(rank - 1 < mine, rank - 1, rank)
        return jnp.where(low, found, depth - 1 - found)

    def forward(p, event, origin, later, onward):
        if onward is not None:
            target_z, inside = onward
            send(p, event, 2, origin, at(target_z, y, x, core), inside)
        for dim in later:
            if dim == "z":
                send(p, event, 2, origin, me - 8, z > 0)
                send(p, event, 3, origin, me + 8, z < depth - 1)
            elif dim == "x":
                send(p, event, 0, origin, at(z, y, 1 - x, core))
            else:
                send(p, event, 1, origin, at(z, 1 - y, x, core))
        send(p, event, 4, origin, at(z, y, x, 1 - core))

    def left_sector(a):
        keep = farthest < ldim_ref[a]
        for t in range(terms):
            lmask[pl.ds(t * extent, extent), :] = jnp.where(
                keep, left_ref[a, t].astype(jnp.float32), 0.0).astype(jnp.bfloat16)

        def one(i, carry):
            k = a * PER_SECTOR + i
            both = jnp.dot(lmask[...], psi[k], preferred_element_type=jnp.float32)
            for t in range(terms):
                lpart[k, :, pl.ds(t * extent, extent)] = both[t * extent:(t + 1) * extent].astype(jnp.bfloat16)
            return carry

        lax.fori_loop(0, PER_SECTOR, one, 0, unroll=4)

    for p, (order, start, count) in enumerate(parts):
        lax.fori_loop(start, start + count, mask_right, 0)
        if p == 0:
            pl.semaphore_wait(barrier, 3 + jnp.where(z > 0, 1, 0) + jnp.where(z < depth - 1, 1, 0))
        forward(p, 0, me, order, None)
    for load in loads[2:]:
        load.wait()

    events = [(rank, dy, dx) for rank in range(depth) for dy in range(2) for dx in range(2)][1:]
    events.sort(key=lambda e: (sum(e), e))
    done = 0
    for number, (rank, dy, dx) in enumerate(events):
        origin_z = other(rank) if rank else z
        origin = at(origin_z, 1 - y if dy else y, 1 - x if dx else x, core)
        for p, (order, _, _) in enumerate(parts):
            differs = {"x": dx, "y": dy, "z": rank}
            arrived = max(i for i, dim in enumerate(order) if differs[dim])
            onward = None
            if order[arrived] == "z":
                below = origin_z < z
                onward = (jnp.where(below, z + 1, z - 1),
                          jnp.where(below, depth - 1 - z, z) > 0)
            wait_arrival(p, origin)
            forward(p, number + 1, origin, order[arrived + 1:], onward)
        if done < sectors:
            left_sector(done)
            done += 1
    for a in range(done, sectors):
        left_sector(a)

    for chip in range(devices // 2):
        for p in range(len(parts)):
            wait_arrival(p, chip * 2 + 1 - core)

    def right(k, carry):
        out_ref[k] = jnp.dot(lpart[k], gathered[sector_ref[k]], preferred_element_type=jnp.float32).astype(jnp.bfloat16)
        return carry

    lax.fori_loop(0, blocks, right, 0, unroll=4)

    for copy, condition in sends:
        if condition is None:
            copy().wait_send()
        else:
            pl.when(condition)(lambda copy=copy: copy().wait_send())


def fused(devices, wavefunction, left_environment, right_environment, right_sector, left_dims, right_dims):
    blocks, extent, _ = wavefunction.shape
    sectors, terms = left_environment.shape[:2]
    height = terms * extent
    parts = len(split_sectors(sectors))
    return pl.pallas_call(
        functools.partial(kernel, devices, terms),
        out_shape=jax.ShapeDtypeStruct((blocks, extent, extent), jnp.bfloat16),
        in_specs=[pl.BlockSpec(memory_space=pl.ANY)] * 6,
        out_specs=pl.BlockSpec(memory_space=pltpu.VMEM),
        scratch_shapes=[
            pltpu.VMEM((devices * sectors, height, extent), jnp.bfloat16),
            pltpu.VMEM((blocks, extent, extent), jnp.bfloat16),
            pltpu.VMEM(left_environment.shape, jnp.bfloat16),
            pltpu.VMEM(right_environment.shape, jnp.bfloat16),
            pltpu.SMEM((blocks,), jnp.int32),
            pltpu.SMEM((sectors,), jnp.int32),
            pltpu.SMEM((sectors,), jnp.int32),
            pltpu.VMEM((height, extent), jnp.bfloat16),
            pltpu.VMEM((blocks, extent, height), jnp.bfloat16),
            pltpu.SemaphoreType.DMA((parts, devices // 2, 5)),
            pltpu.SemaphoreType.DMA((parts, devices)),
            pltpu.SemaphoreType.DMA((6,)),
        ],
        compiler_params=pltpu.CompilerParams(
            collective_id=0, has_side_effects=True, vmem_limit_bytes=VMEM_BYTES),
        cost_estimate=pl.CostEstimate(
            flops=4 * blocks * terms * extent ** 3, transcendentals=0,
            bytes_accessed=4 * blocks * extent * extent),
    )(wavefunction, left_environment, right_environment, right_sector, left_dims, right_dims)


def body(wavefunction, left_environment, right_environment, right_sector, left_dims, right_dims):
    devices = lax.axis_size("blk")
    blocks_here, extent, _ = wavefunction.shape
    sectors_here, terms_here = left_environment.shape[:2]
    needed = 2 * extent * extent * (terms_here * (devices + 1) * sectors_here + (3 + terms_here) * blocks_here)
    if lax.axis_size("term") == 1 and devices % 16 == 0 and sectors_here > 1 and needed < VMEM_BYTES * 3 // 4:
        return fused(devices, wavefunction, left_environment, right_environment, right_sector,
                     left_dims, right_dims)
    right_all = lax.all_gather(square_mask(right_environment, right_dims), "blk", axis=0, tiled=True)
    grouped = wavefunction.reshape(sectors_here, PER_SECTOR, extent, extent)
    left_part = jnp.einsum(
        "atij,apjk->aptik", square_mask(left_environment, left_dims), grouped,
        preferred_element_type=jnp.float32
    )
    left_part = left_part.astype(jnp.bfloat16).reshape(blocks_here, terms_here, extent, extent)
    products = jnp.einsum(
        "ntij,ntjk->nik", left_part, right_all[right_sector], preferred_element_type=jnp.float32
    ).astype(jnp.bfloat16)
    return lax.psum_scatter(products, "term", scatter_dimension=1, tiled=True)


def solution(mesh):
    placed = (
        P(("groups", "blk"), None, None),
        P(("groups", "blk"), "term", None, None),
        P(("groups", "blk"), "term", None, None),
        P(("groups", "blk")),
        P(("groups", "blk")),
        P(("groups", "blk")),
    )
    return jax.shard_map(
        body,
        mesh=mesh,
        in_specs=placed,
        out_specs=P(("groups", "blk"), "term", None),
        check_vma=False,
    )
```

```python
import functools

import jax
import jax.numpy as jnp
from jax import lax
from jax.experimental import pallas as pl
from jax.experimental.pallas import tpu as pltpu
from jax.sharding import PartitionSpec as P

PER_SECTOR = 8
VMEM_BYTES = 50 * 1024 * 1024
ROUTES = (("zyx", 4), ("xzy", 3))


def keep_below(limits, extent):
    return jnp.arange(extent, dtype=jnp.int32)[None, :] < limits[:, None]


def square_mask(operators, limits):
    keep = keep_below(limits, operators.shape[-1])
    keep = keep[:, None, :, None] & keep[:, None, None, :]
    return jnp.where(keep, operators, jnp.zeros((), operators.dtype))


def split_sectors(sectors):
    total = sum(weight for _, weight in ROUTES)
    parts, start, used = [], 0, 0
    for order, weight in ROUTES:
        used += weight
        stop = sectors * used // total
        parts.append((order, start, stop - start))
        start = stop
    return parts


def kernel(devices, terms, psi_hbm, left_hbm, right_hbm, sector_hbm, ldim_hbm, rdim_hbm, out_ref,
           gathered, psi, left_ref, right_ref, sector_ref, ldim_ref, rdim_ref, lmask, lpart,
           send_sem, recv_sem, load_sem):
    sectors, _, extent, _ = right_ref.shape
    blocks = psi.shape[0]
    height = terms * extent
    depth = devices // 8
    me = lax.axis_index("blk")
    core, x, y, z = me % 2, (me // 2) % 2, (me // 4) % 2, me // 8

    def at(zz, yy, xx, cc):
        return zz * 8 + yy * 4 + xx * 2 + cc

    loads = [
        pltpu.make_async_copy(source, target, load_sem.at[i])
        for i, (source, target) in enumerate((
            (rdim_hbm, rdim_ref), (right_hbm, right_ref), (left_hbm, left_ref),
            (psi_hbm, psi), (ldim_hbm, ldim_ref), (sector_hbm, sector_ref)))
    ]
    for load in loads:
        load.start()

    barrier = pltpu.get_barrier_semaphore()
    for peer in (at(z, y, x, 1 - core), at(z, y, 1 - x, core), at(z, 1 - y, x, core)):
        pl.semaphore_signal(barrier, inc=1, device_id={"blk": peer}, device_id_type=pl.DeviceIdType.MESH)

    @pl.when(z > 0)
    def _():
        pl.semaphore_signal(barrier, inc=1, device_id={"blk": me - 8}, device_id_type=pl.DeviceIdType.MESH)

    @pl.when(z < depth - 1)
    def _():
        pl.semaphore_signal(barrier, inc=1, device_id={"blk": me + 8}, device_id_type=pl.DeviceIdType.MESH)

    row_numbers = lax.broadcasted_iota(jnp.int32, (extent, extent), 0)
    col_numbers = lax.broadcasted_iota(jnp.int32, (extent, extent), 1)
    farthest = jnp.maximum(row_numbers, col_numbers)

    for load in loads[:2]:
        load.wait()

    def mask_right(a, carry):
        keep = farthest < rdim_ref[a]
        for t in range(terms):
            gathered[me * sectors + a, pl.ds(t * extent, extent), :] = jnp.where(keep, right_ref[a, t].astype(jnp.float32), 0.0).astype(jnp.bfloat16)
        return carry


    parts = split_sectors(sectors)

    def piece(p, origin):
        _, start, count = parts[p]
        return gathered.at[pl.ds(origin * sectors + start, count)]

    sends = []

    def send(p, event, kind, origin, target, condition=None):
        def copy():
            return pltpu.make_async_remote_copy(
                src_ref=piece(p, origin), dst_ref=piece(p, origin),
                send_sem=send_sem.at[p, event, kind], recv_sem=recv_sem.at[p, origin],
                device_id={"blk": target}, device_id_type=pl.DeviceIdType.MESH)
        if condition is None:
            copy().start()
        else:
            pl.when(condition)(lambda: copy().start())
        sends.append((copy, condition))

    def wait_arrival(p, origin):
        pltpu.make_async_remote_copy(
            src_ref=piece(p, origin), dst_ref=piece(p, origin),
            send_sem=send_sem.at[p, 0, 0], recv_sem=recv_sem.at[p, origin],
            device_id={"blk": at(z, y, x, 1 - core)}, device_id_type=pl.DeviceIdType.MESH).wait_recv()

    def other(rank):
        low = z < depth // 2
        mine = jnp.where(low, z, depth - 1 - z)
        found = jnp.where(rank - 1 < mine, rank - 1, rank)
        return jnp.where(low, found, depth - 1 - found)

    def forward(p, event, origin, later, onward):
        if onward is not None:
            target_z, inside = onward
            send(p, event, 2, origin, at(target_z, y, x, core), inside)
        for dim in later:
            if dim == "z":
                send(p, event, 2, origin, me - 8, z > 0)
                send(p, event, 3, origin, me + 8, z < depth - 1)
            elif dim == "x":
                send(p, event, 0, origin, at(z, y, 1 - x, core))
            else:
                send(p, event, 1, origin, at(z, 1 - y, x, core))
        send(p, event, 4, origin, at(z, y, x, 1 - core))

    def left_sector(a):
        keep = farthest < ldim_ref[a]
        for t in range(terms):
            lmask[pl.ds(t * extent, extent), :] = jnp.where(
                keep, left_ref[a, t].astype(jnp.float32), 0.0).astype(jnp.bfloat16)

        def one(i, carry):
            k = a * PER_SECTOR + i
            both = jnp.dot(lmask[...], psi[k], preferred_element_type=jnp.float32)
            for t in range(terms):
                lpart[k, :, pl.ds(t * extent, extent)] = both[t * extent:(t + 1) * extent].astype(jnp.bfloat16)
            return carry

        lax.fori_loop(0, PER_SECTOR, one, 0, unroll=4)

    for p, (order, start, count) in enumerate(parts):
        lax.fori_loop(start, start + count, mask_right, 0)
        if p == 0:
            pl.semaphore_wait(barrier, 3 + jnp.where(z > 0, 1, 0) + jnp.where(z < depth - 1, 1, 0))
        forward(p, 0, me, order, None)
    for load in loads[2:]:
        load.wait()

    events = [(rank, dy, dx) for rank in range(depth) for dy in range(2) for dx in range(2)][1:]
    events.sort(key=lambda e: (sum(e), -e[0], e))
    done = 0
    for number, (rank, dy, dx) in enumerate(events):
        origin_z = other(rank) if rank else z
        origin = at(origin_z, 1 - y if dy else y, 1 - x if dx else x, core)
        for p, (order, _, _) in enumerate(parts):
            differs = {"x": dx, "y": dy, "z": rank}
            arrived = max(i for i, dim in enumerate(order) if differs[dim])
            onward = None
            if order[arrived] == "z":
                below = origin_z < z
                onward = (jnp.where(below, z + 1, z - 1),
                          jnp.where(below, depth - 1 - z, z) > 0)
            wait_arrival(p, origin)
            forward(p, number + 1, origin, order[arrived + 1:], onward)
        if done < sectors:
            left_sector(done)
            done += 1
    for a in range(done, sectors):
        left_sector(a)

    for chip in range(devices // 2):
        for p in range(len(parts)):
            wait_arrival(p, chip * 2 + 1 - core)

    def right(k, carry):
        out_ref[k] = jnp.dot(lpart[k], gathered[sector_ref[k]], preferred_element_type=jnp.float32).astype(jnp.bfloat16)
        return carry

    lax.fori_loop(0, blocks, right, 0, unroll=4)

    for copy, condition in sends:
        if condition is None:
            copy().wait_send()
        else:
            pl.when(condition)(lambda copy=copy: copy().wait_send())


def fused(devices, wavefunction, left_environment, right_environment, right_sector, left_dims, right_dims):
    blocks, extent, _ = wavefunction.shape
    sectors, terms = left_environment.shape[:2]
    height = terms * extent
    parts = len(split_sectors(sectors))
    return pl.pallas_call(
        functools.partial(kernel, devices, terms),
        out_shape=jax.ShapeDtypeStruct((blocks, extent, extent), jnp.bfloat16),
        in_specs=[pl.BlockSpec(memory_space=pl.ANY)] * 6,
        out_specs=pl.BlockSpec(memory_space=pltpu.VMEM),
        scratch_shapes=[
            pltpu.VMEM((devices * sectors, height, extent), jnp.bfloat16),
            pltpu.VMEM((blocks, extent, extent), jnp.bfloat16),
            pltpu.VMEM(left_environment.shape, jnp.bfloat16),
            pltpu.VMEM(right_environment.shape, jnp.bfloat16),
            pltpu.SMEM((blocks,), jnp.int32),
            pltpu.SMEM((sectors,), jnp.int32),
            pltpu.SMEM((sectors,), jnp.int32),
            pltpu.VMEM((height, extent), jnp.bfloat16),
            pltpu.VMEM((blocks, extent, height), jnp.bfloat16),
            pltpu.SemaphoreType.DMA((parts, devices // 2, 5)),
            pltpu.SemaphoreType.DMA((parts, devices)),
            pltpu.SemaphoreType.DMA((6,)),
        ],
        compiler_params=pltpu.CompilerParams(
            collective_id=0, has_side_effects=True, vmem_limit_bytes=VMEM_BYTES),
        cost_estimate=pl.CostEstimate(
            flops=4 * blocks * terms * extent ** 3, transcendentals=0,
            bytes_accessed=4 * blocks * extent * extent),
    )(wavefunction, left_environment, right_environment, right_sector, left_dims, right_dims)


def body(wavefunction, left_environment, right_environment, right_sector, left_dims, right_dims):
    devices = lax.axis_size("blk")
    blocks_here, extent, _ = wavefunction.shape
    sectors_here, terms_here = left_environment.shape[:2]
    needed = 2 * extent * extent * (terms_here * (devices + 1) * sectors_here + (3 + terms_here) * blocks_here)
    if lax.axis_size("term") == 1 and devices % 16 == 0 and sectors_here > 1 and needed < VMEM_BYTES * 3 // 4:
        return fused(devices, wavefunction, left_environment, right_environment, right_sector,
                     left_dims, right_dims)
    right_all = lax.all_gather(square_mask(right_environment, right_dims), "blk", axis=0, tiled=True)
    grouped = wavefunction.reshape(sectors_here, PER_SECTOR, extent, extent)
    left_part = jnp.einsum(
        "atij,apjk->aptik", square_mask(left_environment, left_dims), grouped,
        preferred_element_type=jnp.float32
    )
    left_part = left_part.astype(jnp.bfloat16).reshape(blocks_here, terms_here, extent, extent)
    products = jnp.einsum(
        "ntij,ntjk->nik", left_part, right_all[right_sector], preferred_element_type=jnp.float32
    ).astype(jnp.bfloat16)
    return lax.psum_scatter(products, "term", scatter_dimension=1, tiled=True)


def solution(mesh):
    placed = (
        P(("groups", "blk"), None, None),
        P(("groups", "blk"), "term", None, None),
        P(("groups", "blk"), "term", None, None),
        P(("groups", "blk")),
        P(("groups", "blk")),
        P(("groups", "blk")),
    )
    return jax.shard_map(
        body,
        mesh=mesh,
        in_specs=placed,
        out_specs=P(("groups", "blk"), "term", None),
        check_vma=False,
    )
```

```python
import functools

import jax
import jax.numpy as jnp
from jax import lax
from jax.experimental import pallas as pl
from jax.experimental.pallas import tpu as pltpu
from jax.sharding import PartitionSpec as P

PER_SECTOR = 8
VMEM_BYTES = 50 * 1024 * 1024
ROUTES = (("zyx", 4), ("xzy", 3))


def keep_below(limits, extent):
    return jnp.arange(extent, dtype=jnp.int32)[None, :] < limits[:, None]


def square_mask(operators, limits):
    keep = keep_below(limits, operators.shape[-1])
    keep = keep[:, None, :, None] & keep[:, None, None, :]
    return jnp.where(keep, operators, jnp.zeros((), operators.dtype))


def split_sectors(sectors):
    total = sum(weight for _, weight in ROUTES)
    parts, start, used = [], 0, 0
    for order, weight in ROUTES:
        used += weight
        stop = sectors * used // total
        parts.append((order, start, stop - start))
        start = stop
    return parts


def kernel(devices, terms, psi_hbm, left_hbm, right_hbm, sector_hbm, ldim_hbm, rdim_hbm, out_ref,
           gathered, psi, left_ref, right_ref, sector_ref, ldim_ref, rdim_ref, lmask, lpart,
           send_sem, recv_sem, load_sem):
    sectors, _, extent, _ = right_ref.shape
    blocks = psi.shape[0]
    height = terms * extent
    depth = devices // 8
    me = lax.axis_index("blk")
    core, x, y, z = me % 2, (me // 2) % 2, (me // 4) % 2, me // 8

    def at(zz, yy, xx, cc):
        return zz * 8 + yy * 4 + xx * 2 + cc

    loads = [
        pltpu.make_async_copy(source, target, load_sem.at[i])
        for i, (source, target) in enumerate((
            (rdim_hbm, rdim_ref), (right_hbm, right_ref), (left_hbm, left_ref),
            (psi_hbm, psi), (ldim_hbm, ldim_ref), (sector_hbm, sector_ref)))
    ]
    for load in loads:
        load.start()

    barrier = pltpu.get_barrier_semaphore()
    for peer in (at(z, y, x, 1 - core), at(z, y, 1 - x, core), at(z, 1 - y, x, core)):
        pl.semaphore_signal(barrier, inc=1, device_id={"blk": peer}, device_id_type=pl.DeviceIdType.MESH)

    @pl.when(z > 0)
    def _():
        pl.semaphore_signal(barrier, inc=1, device_id={"blk": me - 8}, device_id_type=pl.DeviceIdType.MESH)

    @pl.when(z < depth - 1)
    def _():
        pl.semaphore_signal(barrier, inc=1, device_id={"blk": me + 8}, device_id_type=pl.DeviceIdType.MESH)

    row_numbers = lax.broadcasted_iota(jnp.int32, (extent, extent), 0)
    col_numbers = lax.broadcasted_iota(jnp.int32, (extent, extent), 1)
    farthest = jnp.maximum(row_numbers, col_numbers)

    for load in loads[:2]:
        load.wait()

    def mask_right(a, carry):
        keep = farthest < rdim_ref[a]
        for t in range(terms):
            gathered[me * sectors + a, pl.ds(t * extent, extent), :] = jnp.where(keep, right_ref[a, t].astype(jnp.float32), 0.0).astype(jnp.bfloat16)
        return carry


    parts = split_sectors(sectors)

    def piece(p, origin):
        _, start, count = parts[p]
        return gathered.at[pl.ds(origin * sectors + start, count)]

    sends = []

    def send(p, event, kind, origin, target, condition=None):
        def copy():
            return pltpu.make_async_remote_copy(
                src_ref=piece(p, origin), dst_ref=piece(p, origin),
                send_sem=send_sem.at[p, event, kind], recv_sem=recv_sem.at[p, origin],
                device_id={"blk": target}, device_id_type=pl.DeviceIdType.MESH)
        if condition is None:
            copy().start()
        else:
            pl.when(condition)(lambda: copy().start())
        sends.append((copy, condition))

    def wait_arrival(p, origin):
        pltpu.make_async_remote_copy(
            src_ref=piece(p, origin), dst_ref=piece(p, origin),
            send_sem=send_sem.at[p, 0, 0], recv_sem=recv_sem.at[p, origin],
            device_id={"blk": at(z, y, x, 1 - core)}, device_id_type=pl.DeviceIdType.MESH).wait_recv()

    def other(rank):
        low = z < depth // 2
        mine = jnp.where(low, z, depth - 1 - z)
        found = jnp.where(rank - 1 < mine, rank - 1, rank)
        return jnp.where(low, found, depth - 1 - found)

    def forward(p, event, origin, later, onward):
        if onward is not None:
            target_z, inside = onward
            send(p, event, 2, origin, at(target_z, y, x, core), inside)
        for dim in later:
            if dim == "z":
                send(p, event, 2, origin, me - 8, z > 0)
                send(p, event, 3, origin, me + 8, z < depth - 1)
            elif dim == "x":
                send(p, event, 0, origin, at(z, y, 1 - x, core))
            else:
                send(p, event, 1, origin, at(z, 1 - y, x, core))
        send(p, event, 4, origin, at(z, y, x, 1 - core))

    def left_sector(a):
        keep = farthest < ldim_ref[a]
        for t in range(terms):
            lmask[pl.ds(t * extent, extent), :] = jnp.where(
                keep, left_ref[a, t].astype(jnp.float32), 0.0).astype(jnp.bfloat16)

        def one(i, carry):
            k = a * PER_SECTOR + i
            both = jnp.dot(lmask[...], psi[k], preferred_element_type=jnp.float32)
            for t in range(terms):
                lpart[k, :, pl.ds(t * extent, extent)] = both[t * extent:(t + 1) * extent].astype(jnp.bfloat16)
            return carry

        lax.fori_loop(0, PER_SECTOR, one, 0, unroll=8)

    for p, (order, start, count) in enumerate(parts):
        lax.fori_loop(start, start + count, mask_right, 0)
        if p == 0:
            pl.semaphore_wait(barrier, 3 + jnp.where(z > 0, 1, 0) + jnp.where(z < depth - 1, 1, 0))
        forward(p, 0, me, order, None)
    for load in loads[2:]:
        load.wait()

    events = [(rank, dy, dx) for rank in range(depth) for dy in range(2) for dx in range(2)][1:]
    events.sort(key=lambda e: (sum(e), -e[0], e))
    done = 0
    for number, (rank, dy, dx) in enumerate(events):
        origin_z = other(rank) if rank else z
        origin = at(origin_z, 1 - y if dy else y, 1 - x if dx else x, core)
        for p, (order, _, _) in enumerate(parts):
            differs = {"x": dx, "y": dy, "z": rank}
            arrived = max(i for i, dim in enumerate(order) if differs[dim])
            onward = None
            if order[arrived] == "z":
                below = origin_z < z
                onward = (jnp.where(below, z + 1, z - 1),
                          jnp.where(below, depth - 1 - z, z) > 0)
            wait_arrival(p, origin)
            forward(p, number + 1, origin, order[arrived + 1:], onward)
        if done < sectors:
            left_sector(done)
            done += 1
    for a in range(done, sectors):
        left_sector(a)

    for chip in range(devices // 2):
        for p in range(len(parts)):
            wait_arrival(p, chip * 2 + 1 - core)

    def right(k, carry):
        out_ref[k] = jnp.dot(lpart[k], gathered[sector_ref[k]], preferred_element_type=jnp.float32).astype(jnp.bfloat16)
        return carry

    lax.fori_loop(0, blocks, right, 0, unroll=8)

    for copy, condition in sends:
        if condition is None:
            copy().wait_send()
        else:
            pl.when(condition)(lambda copy=copy: copy().wait_send())


def fused(devices, wavefunction, left_environment, right_environment, right_sector, left_dims, right_dims):
    blocks, extent, _ = wavefunction.shape
    sectors, terms = left_environment.shape[:2]
    height = terms * extent
    parts = len(split_sectors(sectors))
    return pl.pallas_call(
        functools.partial(kernel, devices, terms),
        out_shape=jax.ShapeDtypeStruct((blocks, extent, extent), jnp.bfloat16),
        in_specs=[pl.BlockSpec(memory_space=pl.ANY)] * 6,
        out_specs=pl.BlockSpec(memory_space=pltpu.VMEM),
        scratch_shapes=[
            pltpu.VMEM((devices * sectors, height, extent), jnp.bfloat16),
            pltpu.VMEM((blocks, extent, extent), jnp.bfloat16),
            pltpu.VMEM(left_environment.shape, jnp.bfloat16),
            pltpu.VMEM(right_environment.shape, jnp.bfloat16),
            pltpu.SMEM((blocks,), jnp.int32),
            pltpu.SMEM((sectors,), jnp.int32),
            pltpu.SMEM((sectors,), jnp.int32),
            pltpu.VMEM((height, extent), jnp.bfloat16),
            pltpu.VMEM((blocks, extent, height), jnp.bfloat16),
            pltpu.SemaphoreType.DMA((parts, devices // 2, 5)),
            pltpu.SemaphoreType.DMA((parts, devices)),
            pltpu.SemaphoreType.DMA((6,)),
        ],
        compiler_params=pltpu.CompilerParams(
            collective_id=0, has_side_effects=True, vmem_limit_bytes=VMEM_BYTES),
        cost_estimate=pl.CostEstimate(
            flops=4 * blocks * terms * extent ** 3, transcendentals=0,
            bytes_accessed=4 * blocks * extent * extent),
    )(wavefunction, left_environment, right_environment, right_sector, left_dims, right_dims)


def body(wavefunction, left_environment, right_environment, right_sector, left_dims, right_dims):
    devices = lax.axis_size("blk")
    blocks_here, extent, _ = wavefunction.shape
    sectors_here, terms_here = left_environment.shape[:2]
    needed = 2 * extent * extent * (terms_here * (devices + 1) * sectors_here + (3 + terms_here) * blocks_here)
    if lax.axis_size("term") == 1 and devices % 16 == 0 and sectors_here > 1 and needed < VMEM_BYTES * 3 // 4:
        return fused(devices, wavefunction, left_environment, right_environment, right_sector,
                     left_dims, right_dims)
    right_all = lax.all_gather(square_mask(right_environment, right_dims), "blk", axis=0, tiled=True)
    grouped = wavefunction.reshape(sectors_here, PER_SECTOR, extent, extent)
    left_part = jnp.einsum(
        "atij,apjk->aptik", square_mask(left_environment, left_dims), grouped,
        preferred_element_type=jnp.float32
    )
    left_part = left_part.astype(jnp.bfloat16).reshape(blocks_here, terms_here, extent, extent)
    products = jnp.einsum(
        "ntij,ntjk->nik", left_part, right_all[right_sector], preferred_element_type=jnp.float32
    ).astype(jnp.bfloat16)
    return lax.psum_scatter(products, "term", scatter_dimension=1, tiled=True)


def solution(mesh):
    placed = (
        P(("groups", "blk"), None, None),
        P(("groups", "blk"), "term", None, None),
        P(("groups", "blk"), "term", None, None),
        P(("groups", "blk")),
        P(("groups", "blk")),
        P(("groups", "blk")),
    )
    return jax.shard_map(
        body,
        mesh=mesh,
        in_specs=placed,
        out_specs=P(("groups", "blk"), "term", None),
        check_vma=False,
    )
```
